32 devices in a mesh: ens: 2 (over y), curve: 8 (over z, x), sub: 2 (over core).
Axes of the slice: x: 2, y: 2, z: 4, core: 2. Of those that a mesh axis runs over, the one named last changes fastest.
Arguments:
- conductivity: float32 [256, 4096], P(('ens', 'curve', 'sub')), parts along dimension 0, may hold values from 0.01 to 27
- neighbours: int32 [6, 256], P(None, ('ens', 'curve', 'sub')), parts along dimension 1, may hold values from -1 to 127, as said below
- live_count: int32 [32], P(('ens', 'curve', 'sub')), parts along dimension 0, may hold values from 0 to 8, as said below
Outputs:
- solution_field: float32 [3, 256, 4096], P(None, ('ens', 'curve', 'sub')), parts along dimension 1
- residual: float32 [3, 256, 4096], P(None, ('ens', 'curve', 'sub')), parts along dimension 1
The draws below stay inside these ranges and needn't reach their ends.
There are 2 independent parts, one for each index of `ens`. The reference program is written for one: setup_inputs(seed, part) draws one part's arguments, and reference() takes and returns one part's arrays. A program takes and returns all parts, laid end to end along the dimension named above; each array names one. Nothing has to cross between parts.
Inputs may be any that keep to these rules, and one draw needn't show every extreme that they name: `live_count`: active bricks of a device fill its slots 0 to count - 1; some device has 8. Entries of empty slots are -1. The relation is symmetric across opposite sides. A -x or +x neighbour lies on the same device or on the device one before or one after along curve+sub, on the side named; all other neighbours lie on the same device. At most 4 bricks of a device have a +x neighbour on the next device, and some device reaches it.
All inputs are finite; a program needn't handle non-finite values.
Results may differ from the reference program's by a relative error of at most 0.00019.
Values sent between devices are 32-bit elements; how exact they have to be, the bound alone decides.
A program may use at most 64 MiB of HBM per device.

```python
import math
import jax
import jax.numpy as jnp
import numpy as np
from jax import lax

BRICK_EDGE_VOXELS = 16
LEVELS = 1
ITERS = 4
DEVICE_SLOTS = 8
GROUP = 16
GROUP_SLOT_COUNT = 128


HILBERT_POS = np.array([[[0, 3, 4, 5], [1, 2, 7, 6]], [[6, 5, 0, 1], [7, 4, 3, 2]]], dtype=np.int32)


def brick_geometry(key):
    width = 2 * GROUP
    grid_key, pick_key = jax.random.split(key)
    active_bricks = jax.random.randint(grid_key, (width, 4, LEVELS), 0, 10) < 7
    first = jax.random.randint(pick_key, (), 0, GROUP - 1)
    column = jnp.arange(width, dtype=jnp.int32)
    owner_device = column // 2
    forced = (owner_device == first) | (owner_device == first + 1)
    active_bricks = active_bricks | forced[:, None, None]
    table = jnp.asarray(HILBERT_POS)
    order = table[(owner_device % 2)[:, None], (column % 2)[:, None], jnp.arange(4, dtype=jnp.int32)[None, :]]
    rank_key = order[:, :, None] * LEVELS + jnp.arange(LEVELS, dtype=jnp.int32)[None, None, :]
    owner_grid = jnp.broadcast_to(owner_device[:, None, None], rank_key.shape)
    filled = jnp.zeros((GROUP, DEVICE_SLOTS), jnp.int32).at[owner_grid, rank_key].set(active_bricks.astype(jnp.int32))
    ranks = jnp.cumsum(filled, axis=1) - 1
    counts = jnp.sum(filled, axis=1).astype(jnp.int32)
    global_slot_number = jnp.where(active_bricks, owner_grid * DEVICE_SLOTS + ranks[owner_grid, rank_key], -1).astype(jnp.int32)
    padded = jnp.pad(global_slot_number, 1, constant_values=-1)
    sides = [padded[:-2, 1:-1, 1:-1], padded[2:, 1:-1, 1:-1], padded[1:-1, :-2, 1:-1], padded[1:-1, 2:, 1:-1], padded[1:-1, 1:-1, :-2], padded[1:-1, 1:-1, 2:]]
    value_entries = jnp.stack([plane.reshape(-1) for plane in sides])
    target_slots = jnp.where(active_bricks, global_slot_number, GROUP_SLOT_COUNT).reshape(-1)
    result_field = jnp.full((6, GROUP_SLOT_COUNT), -1, jnp.int32).at[:, target_slots].set(value_entries, mode='drop')
    return (result_field, counts)


def draw_neighbours(key, part):
    result_field, counts = brick_geometry(jax.random.fold_in(key, 7))
    return result_field


def draw_live_count(key, part):
    result_field, counts = brick_geometry(jax.random.fold_in(key, 7))
    return counts


def draw_conductivity(key, part):
    pore_key, high_key, low_key = jax.random.split(jax.random.fold_in(key, 11), 3)
    array_shape = (GROUP_SLOT_COUNT, BRICK_EDGE_VOXELS ** 3)
    owner_device = (jnp.arange(GROUP_SLOT_COUNT, dtype=jnp.int32) // DEVICE_SLOTS).astype(jnp.float32)
    position = owner_device / max(GROUP - 1, 1)
    pore = jax.random.uniform(pore_key, array_shape) < 0.6
    pore_value = jnp.exp(jax.random.uniform(high_key, array_shape, minval=math.log(0.5), maxval=math.log(2.0)))
    solid_value = jnp.exp(jax.random.uniform(low_key, array_shape, minval=math.log(0.02), maxval=math.log(0.08)))
    ramp = jnp.exp(math.log(3.0) * position)
    return (jnp.where(pore, pore_value, solid_value) * ramp[:, None]).astype(jnp.float32)


def setup_inputs(seed: int = 0, part: int = 0) -> dict:
    key_of = jax.random.split(jax.random.key(seed), 4)
    part_splits = jax.random.split(jax.random.fold_in(key_of[3], part), 4)
    return {
        "conductivity": draw_conductivity(jax.random.fold_in(jax.random.fold_in(key_of[3], part), 71), part),
        "neighbours": draw_neighbours(jax.random.fold_in(jax.random.fold_in(key_of[3], part), 71), part),
        "live_count": draw_live_count(jax.random.fold_in(jax.random.fold_in(key_of[3], part), 71), part),
    }


def normal_axis(side):
    return (2, 2, 1, 1, 0, 0)[side]


def face_layer(field, side, brick):
    lead = field.shape[:-1]
    cube = field.reshape(lead + (brick, brick, brick))
    axis = len(lead) + normal_axis(side)
    place = 0 if side % 2 == 0 else brick - 1
    layer = lax.index_in_dim(cube, place, axis=axis, keepdims=False)
    return layer.reshape(lead + (brick * brick,))


def spread_face(face, side, brick):
    lead = face.shape[:-1]
    plane = face.reshape(lead + (brick, brick))
    axis = len(lead) + normal_axis(side)
    cube = jnp.broadcast_to(jnp.expand_dims(plane, axis), lead + (brick, brick, brick))
    return cube.reshape(lead + (brick ** 3,))


def inner_shift(field, side, brick):
    lead = field.shape[:-1]
    cube = field.reshape(lead + (brick, brick, brick))
    axis = len(lead) + normal_axis(side)
    blank = jnp.zeros_like(lax.slice_in_dim(cube, 0, 1, axis=axis))
    if side % 2 == 0:
        moved = jnp.concatenate([blank, lax.slice_in_dim(cube, 0, brick - 1, axis=axis)], axis)
    else:
        moved = jnp.concatenate([lax.slice_in_dim(cube, 1, brick, axis=axis), blank], axis)
    return moved.reshape(lead + (brick ** 3,))


def edge_mask(side, brick):
    voxel = jnp.arange(brick ** 3, dtype=jnp.int32)
    coords = (voxel // (brick * brick), (voxel // brick) % brick, voxel % brick)
    target = 0 if side % 2 == 0 else brick - 1
    return coords[normal_axis(side)] == target


def beside_value(field, face, side, brick):
    return jnp.where(edge_mask(side, brick), spread_face(face, side, brick), inner_shift(field, side, brick))


def picked_faces(field, neighbours, keep_own):
    faces = []
    for side in range(6):
        layers = face_layer(field, side ^ 1, BRICK_EDGE_VOXELS)
        index = neighbours[side]
        valid = index >= 0
        picked = jnp.take(layers, jnp.maximum(index, 0), axis=layers.ndim - 2)
        fill = face_layer(field, side, BRICK_EDGE_VOXELS) if keep_own else jnp.float32(0.0)
        faces.append(jnp.where(valid[:, None], picked, fill))
    return faces


def apply_operator(field, neighbours, weights, diagonal):
    faces = picked_faces(field, neighbours, False)
    result_field = diagonal * field
    for side in range(6):
        result_field = result_field - weights[side] * beside_value(field, faces[side], side, BRICK_EDGE_VOXELS)
    return result_field


def reference(conductivity, neighbours, live_count):
    slot_position_index = jnp.arange(GROUP_SLOT_COUNT, dtype=jnp.int32)
    live = (slot_position_index % DEVICE_SLOTS) < live_count[slot_position_index // DEVICE_SLOTS]
    faces = picked_faces(conductivity, neighbours, True)
    weights = []
    for side in range(6):
        other = beside_value(conductivity, faces[side], side, BRICK_EDGE_VOXELS)
        weights.append(jnp.where(live[:, None], 2.0 * conductivity * other / (conductivity + other), 0.0))
    total = weights[0]
    for side in range(1, 6):
        total = total + weights[side]
    diagonal = jnp.where(live[:, None], total, 1.0)
    rhs = jnp.stack([weights[1] - weights[0], weights[3] - weights[2], weights[5] - weights[4]])
    solution_field = jnp.zeros_like(rhs)
    residual = rhs
    scaled = residual / diagonal
    direction = scaled
    current = jnp.sum(residual * scaled, axis=(1, 2))
    for step in range(ITERS):
        image = apply_operator(direction, neighbours, weights, diagonal)
        alpha = current / jnp.sum(direction * image, axis=(1, 2))
        solution_field = solution_field + alpha[:, None, None] * direction
        residual = residual - alpha[:, None, None] * image
        if step + 1 < ITERS:
            scaled = residual / diagonal
            fresh = jnp.sum(residual * scaled, axis=(1, 2))
            direction = scaled + (fresh / current)[:, None, None] * direction
            current = fresh
    return solution_field, residual
```

```python
import functools

import jax
import jax.numpy as jnp
from jax import lax
from jax.experimental import pallas as pl
from jax.experimental.pallas import tpu as pltpu
from jax.sharding import PartitionSpec as P

EDGE = 16
ITERS = 4
LANES = 128
SLOTS = 8
TILES = EDGE**3 // LANES
HALF = EDGE // 2
MOMENTS = 2 * ITERS
MESH = pl.DeviceIdType.MESH


def pick(tile, index):
    return jnp.take_along_axis(tile, index, axis=0, mode="promise_in_bounds")


def total_of(terms):
    terms = list(terms)
    while len(terms) > 1:
        terms = [
            terms[i] + terms[i + 1] if i + 1 < len(terms) else terms[i]
            for i in range(0, len(terms), 2)
        ]
    return terms[0]


def cg_coefficients(nu):
    def gram(i, j):
        return 0.5 * (nu[i + j] + nu[abs(i - j)])

    def pair(a, b):
        return total_of(x * y * gram(i, j) for i, x in enumerate(a) for j, y in enumerate(b))

    def image_of(p):
        q = list(p) + [jnp.zeros_like(p[0])]
        for j, x in enumerate(p):
            if j == 0:
                q[1] = q[1] - x
            else:
                q[j + 1] = q[j + 1] - 0.5 * x
                q[j - 1] = q[j - 1] - 0.5 * x
        return q

    scaled = [jnp.ones_like(nu[0])]
    direction = list(scaled)
    iterate = []
    current = nu[0]
    for step in range(ITERS):
        image = image_of(direction)
        alpha = current / pair(direction, image)
        iterate = [
            (iterate[i] + alpha * x) if i < len(iterate) else alpha * x
            for i, x in enumerate(direction)
        ]
        scaled = [
            (scaled[i] - alpha * x) if i < len(scaled) else -alpha * x
            for i, x in enumerate(image)
        ]
        if step + 1 < ITERS:
            fresh = pair(scaled, scaled)
            beta = fresh / current
            direction = [
                x + beta * direction[i] if i < len(direction) else x
                for i, x in enumerate(scaled)
            ]
            current = fresh
    return iterate, scaled


def kernel(
    peers, subs, k_ref, nb_ref, live_ref, x_ref, r_ref,
    kp, field, weight, diag, link, faces, ghosts, fix, edge_w, moments, gathered,
    face_send, face_recv, sum_send, sum_recv,
):
    me = lax.axis_index("curve") * subs + lax.axis_index("sub")

    def device(index):
        return {"curve": index // subs, "sub": lax.rem(index, subs)}

    barrier = pltpu.get_barrier_semaphore()

    def greet(offset, carry):
        pl.semaphore_signal(
            barrier, inc=1, device_id=device(lax.rem(me + offset, peers)), device_id_type=MESH
        )
        return carry

    lax.fori_loop(1, peers, greet, 0)

    shape = (SLOTS, LANES)
    lane = lax.broadcasted_iota(jnp.int32, shape, 1)
    slot = lax.broadcasted_iota(jnp.int32, shape, 0)
    column = lane % EDGE
    first_x, last_x = column == 0, column == EDGE - 1
    first_y, last_y = lane < EDGE, lane >= LANES - EDGE
    live = slot < live_ref[0]
    index, valid, remote = [], [], []
    for side in range(6):
        entry = jnp.full(shape, nb_ref[side, 0], jnp.int32)
        for s in range(1, SLOTS):
            entry = jnp.where(slot == s, nb_ref[side, s], entry)
        valid.append(entry >= 0)
        index.append(jnp.where(valid[side], entry % SLOTS, 0))
        if side < 2:
            remote.append(
                valid[side] & ((entry < me * SLOTS) | (entry >= (me + 1) * SLOTS))
            )

    def copies(step, width):
        def make(side, peer):
            span = pl.ds(0, width)
            return pltpu.make_async_remote_copy(
                src_ref=faces.at[step, side, span],
                dst_ref=ghosts.at[step, 1 - side, span],
                send_sem=face_send.at[step, side],
                recv_sem=face_recv.at[step, 1 - side],
                device_id=device(peer),
                device_id_type=MESH,
            )

        return make(0, jnp.maximum(me - 1, 0)), make(1, jnp.minimum(me + 1, peers - 1))

    def send(step, width):
        down, up = copies(step, width)

        @pl.when(me > 0)
        def _():
            down.start()

        @pl.when(me < peers - 1)
        def _():
            up.start()

    def receive(step, width):
        down, up = copies(step, width)

        @pl.when(me < peers - 1)
        def _():
            down.wait_recv()
            up.wait_send()

        @pl.when(me > 0)
        def _():
            up.wait_recv()
            down.wait_send()

    def compact(tile, side, place, into):
        turn = place if side == 0 else place + LANES - (EDGE - 1)
        return jnp.where(column == place, pltpu.roll(tile, lax.rem(turn, LANES), 1), into)

    def spread(tile, side, place):
        turn = (LANES - place) if side == 0 else (EDGE - 1) - place
        return pltpu.roll(tile, lax.rem(turn + LANES, LANES), 1)

    def ghost(step, side, comp, half):
        near = pick(faces[step, 1 - side, comp, half], index[side])
        far = pick(ghosts[step, side, comp, half], index[side])
        return jnp.where(remote[side], far, near)

    def shifts_y(pair):
        low = [pltpu.roll(tile, EDGE, 1) for tile in pair]
        high = [pltpu.roll(tile, LANES - EDGE, 1) for tile in pair]
        before = [
            jnp.where(first_y, pick(low[1], index[2]), low[0]),
            jnp.where(first_y, low[0], low[1]),
        ]
        after = [
            jnp.where(last_y, high[1], high[0]),
            jnp.where(last_y, pick(high[0], index[3]), high[1]),
        ]
        return before, after

    zero = jnp.zeros(shape, jnp.float32)

    for half in range(2):
        low, high = zero, zero
        for p in range(EDGE):
            t = half * EDGE + p
            tile = k_ref[:, t * LANES : (t + 1) * LANES]
            kp[2 + t] = tile
            low = compact(tile, 0, p, low)
            high = compact(tile, 1, p, high)
        faces[0, 0, 0, half] = low
        faces[0, 1, 0, half] = high
    for h in range(2):
        kp[h] = jnp.where(valid[4], pick(kp[TILES + h], index[4]), kp[2 + h])
        kp[TILES + 2 + h] = jnp.where(valid[5], pick(kp[2 + h], index[5]), kp[TILES + h])

    pl.semaphore_wait(barrier, peers - 1)
    send(0, 1)

    def harmonic(a, b):
        return jnp.where(live, 2.0 * a * b / (a + b), 0.0)

    def links(z, carry):
        pair = [kp[2 + 2 * z + h] for h in range(2)]
        before, after = shifts_y(pair)
        before[0] = jnp.where(first_y & ~valid[2], pair[0], before[0])
        after[1] = jnp.where(last_y & ~valid[3], pair[1], after[1])
        for h in range(2):
            t = 2 * z + h
            k = pair[h]
            link[0, t] = jnp.where(first_x, 0.0, harmonic(k, pltpu.roll(k, 1, 1)))
            link[1, t] = jnp.where(last_x, 0.0, harmonic(k, pltpu.roll(k, LANES - 1, 1)))
            link[2, t] = harmonic(k, before[h])
            link[3, t] = harmonic(k, after[h])
            link[4, t] = harmonic(k, kp[t])
            link[5, t] = harmonic(k, kp[t + 4])
        return carry

    lax.fori_loop(0, EDGE, links, 0)
    receive(0, 1)

    for side in range(2):
        for half in range(2):
            own = faces[0, side, 0, half]
            other = jnp.where(valid[side], ghost(0, side, 0, half), own)
            fix[side, 0, half] = harmonic(own, other)

    def finish_faces(step, half, found):
        for side in range(2):
            for comp in range(3):
                faces[step, side, comp, half] = found[side * 3 + comp]

    for half in range(2):

        def start(row, carry, half=half):
            carry = list(carry)
            for h in range(2):
                p = 2 * row + h
                t = half * EDGE + p
                w = [link[side, t] for side in range(6)]
                w[0] = jnp.where(first_x, spread(fix[0, 0, half], 0, p), w[0])
                w[1] = jnp.where(last_x, spread(fix[1, 0, half], 1, p), w[1])
                total = ((((w[0] + w[1]) + w[2]) + w[3]) + w[4]) + w[5]
                d = jnp.where(live, total, 1.0)
                inverse = 1.0 / d
                diag[t] = d
                n = [x * inverse for x in w]
                if h == 0:
                    n[2] = jnp.where(first_y & ~valid[2], 0.0, n[2])
                if h == 1:
                    n[3] = jnp.where(last_y & ~valid[3], 0.0, n[3])
                weight[0, t] = jnp.where(first_x, 0.0, n[0])
                weight[1, t] = jnp.where(last_x, 0.0, n[1])
                for side in range(2, 6):
                    weight[side, t] = n[side]
                for comp in range(3):
                    v = (w[2 * comp + 1] - w[2 * comp]) * inverse
                    field[0, comp, 2 + t] = v
                    carry[comp] = compact(v, 0, p, carry[comp])
                    carry[3 + comp] = compact(v, 1, p, carry[3 + comp])
                carry[6] = compact(n[0], 0, p, carry[6])
                carry[7] = compact(n[1], 1, p, carry[7])
            return tuple(carry)

        found = lax.fori_loop(0, HALF, start, (zero,) * 8)
        finish_faces(1, half, found)
        edge_w[0, half] = jnp.where(valid[0], found[6], 0.0)
        edge_w[1, half] = jnp.where(valid[1], found[7], 0.0)

    sums = []
    for j in range(ITERS):
        if j == 0:
            send(1, 3)
        for comp in range(3):
            for h in range(2):
                field[j, comp, h] = jnp.where(
                    valid[4], pick(field[j, comp, TILES + h], index[4]), 0.0
                )
                field[j, comp, TILES + 2 + h] = jnp.where(
                    valid[5], pick(field[j, comp, 2 + h], index[5]), 0.0
                )
        for half in range(2):

            def inner(row, carry, half=half, j=j):
                carry = list(carry)
                base = half * EDGE + 2 * row
                w = [[weight[side, base + h] for side in range(6)] for h in range(2)]
                for comp in range(3):
                    pair = [field[j, comp, 2 + base + h] for h in range(2)]
                    before, after = shifts_y(pair)
                    for h in range(2):
                        t = base + h
                        p = 2 * row + h
                        u = pair[h]
                        value = (
                            (w[h][0] * pltpu.roll(u, 1, 1) + w[h][1] * pltpu.roll(u, LANES - 1, 1))
                            + (w[h][2] * before[h] + w[h][3] * after[h])
                            + (w[h][4] * field[j, comp, t] + w[h][5] * field[j, comp, t + 4])
                        )
                        if j > 0:
                            value = 2.0 * value - field[j - 1, comp, 2 + t]
                        field[j + 1, comp, 2 + t] = value
                        if j + 1 < ITERS:
                            carry[comp] = compact(value, 0, p, carry[comp])
                            carry[3 + comp] = compact(value, 1, p, carry[3 + comp])
                return tuple(carry)

            found = lax.fori_loop(0, HALF, inner, (zero,) * 6)
            if j + 1 < ITERS:
                finish_faces(j + 2, half, found)
        receive(j + 1, 3)
        for half in range(2):
            for side in range(2):
                w = edge_w[side, half]
                if j > 0:
                    w = 2.0 * w
                for comp in range(3):
                    extra = jnp.where(valid[side], w * ghost(j + 1, side, comp, half), 0.0)
                    fix[side, comp, half] = extra
                    if j + 1 < ITERS:
                        faces[j + 2, side, comp, half] = faces[j + 2, side, comp, half] + extra
        if j + 1 < ITERS:
            send(j + 2, 3)

        accumulated = (zero,) * 6
        for half in range(2):

            def outer(row, carry, half=half, j=j):
                carry = list(carry)
                for h in range(2):
                    p = 2 * row + h
                    t = half * EDGE + p
                    d = diag[t]
                    for comp in range(3):
                        value = field[j + 1, comp, 2 + t]
                        value = value + jnp.where(
                            first_x,
                            spread(fix[0, comp, half], 0, p),
                            jnp.where(last_x, spread(fix[1, comp, half], 1, p), 0.0),
                        )
                        field[j + 1, comp, 2 + t] = value
                        old = field[j, comp, 2 + t]
                        scaled = d * old
                        carry[comp] = carry[comp] + scaled * old
                        carry[3 + comp] = carry[3 + comp] + scaled * value
                return tuple(carry)

            accumulated = lax.fori_loop(0, HALF, outer, accumulated)
        sums.append(accumulated)

    mine = zero
    for comp in range(3):
        rows = zero
        for j in range(ITERS):
            for odd in range(2):
                row = jnp.sum(sums[j][3 * odd + comp], axis=0, keepdims=True)
                rows = jnp.where(slot == 2 * j + odd, row, rows)
        mine = jnp.where(lane == comp, jnp.sum(rows, axis=1, keepdims=True), mine)
    moments[...] = mine
    gathered[me] = mine

    def share(offset):
        peer = lax.rem(me + offset, peers)
        return pltpu.make_async_remote_copy(
            src_ref=moments,
            dst_ref=gathered.at[me],
            send_sem=sum_send.at[offset],
            recv_sem=sum_recv.at[me],
            device_id=device(peer),
            device_id_type=MESH,
        )

    def launch(offset, carry):
        share(offset).start()
        return carry

    lax.fori_loop(1, peers, launch, 0)

    def collect(offset, carry):
        source = lax.rem(me + offset, peers)
        share(offset).wait_send()
        pltpu.make_async_remote_copy(
            src_ref=moments,
            dst_ref=gathered.at[source],
            send_sem=sum_send.at[offset],
            recv_sem=sum_recv.at[source],
            device_id=device(source),
            device_id_type=MESH,
        ).wait_recv()
        return carry

    lax.fori_loop(1, peers, collect, 0)
    whole = jnp.sum(gathered[...], axis=0)

    rows = [whole[m : m + 1, :] for m in range(MOMENTS)]
    nu = rows[:2]
    for m in range(2, MOMENTS):
        nu.append(2.0 * rows[m] - rows[m % 2])
    iterate, scaled = cg_coefficients(nu)

    def over(row, comp):
        return jnp.broadcast_to(row[:, comp : comp + 1], shape)

    for comp in range(3):
        a = [over(row, comp) for row in iterate]
        b = [over(row, comp) for row in scaled]
        for t in range(TILES):
            v = [field[j, comp, 2 + t] for j in range(ITERS + 1)]
            span = slice(t * LANES, (t + 1) * LANES)
            x_ref[comp, :, span] = total_of(a[j] * v[j] for j in range(ITERS))
            r_ref[comp, :, span] = diag[t] * total_of(b[j] * v[j] for j in range(ITERS + 1))


def local(peers, subs, conductivity, neighbours, live_count):
    slots, voxels = conductivity.shape
    out = jax.ShapeDtypeStruct((3, slots, voxels), jnp.float32)
    vmem = pl.BlockSpec(memory_space=pltpu.VMEM)
    smem = pl.BlockSpec(memory_space=pltpu.SMEM)
    tile = (SLOTS, LANES)
    return pl.pallas_call(
        functools.partial(kernel, peers, subs),
        out_shape=(out, out),
        in_specs=[vmem, smem, smem],
        out_specs=(vmem, vmem),
        scratch_shapes=[
            pltpu.VMEM((TILES + 4, *tile), jnp.float32),
            pltpu.VMEM((ITERS + 1, 3, TILES + 4, *tile), jnp.float32),
            pltpu.VMEM((6, TILES, *tile), jnp.float32),
            pltpu.VMEM((TILES, *tile), jnp.float32),
            pltpu.VMEM((6, TILES, *tile), jnp.float32),
            pltpu.VMEM((ITERS + 1, 2, 3, 2, *tile), jnp.float32),
            pltpu.VMEM((ITERS + 1, 2, 3, 2, *tile), jnp.float32),
            pltpu.VMEM((2, 3, 2, *tile), jnp.float32),
            pltpu.VMEM((2, 2, *tile), jnp.float32),
            pltpu.VMEM(tile, jnp.float32),
            pltpu.VMEM((peers, *tile), jnp.float32),
            pltpu.SemaphoreType.DMA((ITERS + 1, 2)),
            pltpu.SemaphoreType.DMA((ITERS + 1, 2)),
            pltpu.SemaphoreType.DMA((peers,)),
            pltpu.SemaphoreType.DMA((peers,)),
        ],
        compiler_params=pltpu.CompilerParams(
            collective_id=0, has_side_effects=True, vmem_limit_bytes=24 * 1024 * 1024
        ),
    )(conductivity, neighbours, live_count)


def solution(mesh):
    names = ("ens", "curve", "sub")
    peers = mesh.shape["curve"] * mesh.shape["sub"]
    in_specs = (P(names, None), P(None, names), P(names))
    out_specs = (P(None, names, None), P(None, names, None))
    return jax.shard_map(
        functools.partial(local, peers, mesh.shape["sub"]),
        mesh=mesh, in_specs=in_specs, out_specs=out_specs, check_vma=False,
    )
```

```python
import functools

import jax
import jax.numpy as jnp
from jax import lax
from jax.experimental import pallas as pl
from jax.experimental.pallas import tpu as pltpu
from jax.sharding import PartitionSpec as P

EDGE = 16
ITERS = 4
LANES = 128
SLOTS = 8
MOMENTS = 2 * ITERS
MESH = pl.DeviceIdType.MESH


def total_of(terms):
    terms = list(terms)
    while len(terms) > 1:
        terms = [
            terms[i] + terms[i + 1] if i + 1 < len(terms) else terms[i]
            for i in range(0, len(terms), 2)
        ]
    return terms[0]


def cg_coefficients(nu):
    def gram(i, j):
        return 0.5 * (nu[i + j] + nu[abs(i - j)])

    def pair(a, b):
        return total_of(x * y * gram(i, j) for i, x in enumerate(a) for j, y in enumerate(b))

    def image_of(p):
        q = list(p) + [jnp.zeros_like(p[0])]
        for j, x in enumerate(p):
            if j == 0:
                q[1] = q[1] - x
            else:
                q[j + 1] = q[j + 1] - 0.5 * x
                q[j - 1] = q[j - 1] - 0.5 * x
        return q

    scaled = [jnp.ones_like(nu[0])]
    direction = list(scaled)
    iterate = []
    current = nu[0]
    for step in range(ITERS):
        image = image_of(direction)
        alpha = current / pair(direction, image)
        iterate = [
            (iterate[i] + alpha * x) if i < len(iterate) else alpha * x
            for i, x in enumerate(direction)
        ]
        scaled = [
            (scaled[i] - alpha * x) if i < len(scaled) else -alpha * x
            for i, x in enumerate(image)
        ]
        if step + 1 < ITERS:
            fresh = pair(scaled, scaled)
            beta = fresh / current
            direction = [
                x + beta * direction[i] if i < len(direction) else x
                for i, x in enumerate(scaled)
            ]
            current = fresh
    return iterate, scaled


def kernel(
    peers, subs, k_ref, nb_ref, live_ref, x_ref, r_ref,
    kp, field, weight, diag, link, faces, ghosts, edge_w, turned, moments, gathered,
    face_send, face_recv, sum_send, sum_recv,
):
    me = lax.axis_index("curve") * subs + lax.axis_index("sub")

    def device(index):
        return {"curve": index // subs, "sub": lax.rem(index, subs)}

    barrier = pltpu.get_barrier_semaphore()

    def greet(offset, carry):
        pl.semaphore_signal(
            barrier, inc=1, device_id=device(lax.rem(me + offset, peers)), device_id_type=MESH
        )
        return carry

    lax.fori_loop(1, peers, greet, 0)

    shape = (EDGE, LANES)
    lane = lax.broadcasted_iota(jnp.int32, shape, 1)
    row = lax.broadcasted_iota(jnp.int32, shape, 0)
    depth = lane % EDGE
    owner = lane // EDGE
    first_x, last_x = row == 0, row == EDGE - 1
    first_z, last_z = depth == 0, depth == EDGE - 1
    live = owner < live_ref[0]
    index, valid, remote = [], [], []
    for side in range(6):
        entry = jnp.full(shape, nb_ref[side, 0], jnp.int32)
        for s in range(1, SLOTS):
            entry = jnp.where(owner == s, nb_ref[side, s], entry)
        valid.append(entry >= 0)
        index.append(jnp.where(valid[side], entry % SLOTS, 0) * EDGE)
        if side < 2:
            remote.append(
                valid[side] & ((entry < me * SLOTS) | (entry >= (me + 1) * SLOTS))
            )
    for side in range(4):
        index[side] = index[side] + depth
    index[4] = jnp.where(first_z, index[4] + (EDGE - 1), lane - 1)
    index[5] = jnp.where(last_z, index[5], lane + 1)

    def pick(block, side):
        where = index[side]
        return jnp.concatenate(
            [
                jnp.take_along_axis(
                    block[h : h + 8], where[h : h + 8], axis=1, mode="promise_in_bounds"
                )
                for h in range(0, EDGE, 8)
            ],
            axis=0,
        )

    def copies(step, width):
        def make(side, peer):
            span = pl.ds(0, width)
            return pltpu.make_async_remote_copy(
                src_ref=faces.at[step, side, span],
                dst_ref=ghosts.at[step, 1 - side, span],
                send_sem=face_send.at[step, side],
                recv_sem=face_recv.at[step, 1 - side],
                device_id=device(peer),
                device_id_type=MESH,
            )

        return make(0, jnp.maximum(me - 1, 0)), make(1, jnp.minimum(me + 1, peers - 1))

    def send(step, width):
        down, up = copies(step, width)

        @pl.when(me > 0)
        def _():
            down.start()

        @pl.when(me < peers - 1)
        def _():
            up.start()

    def receive(step, width):
        down, up = copies(step, width)

        @pl.when(me < peers - 1)
        def _():
            down.wait_recv()
            up.wait_send()

        @pl.when(me > 0)
        def _():
            up.wait_recv()
            down.wait_send()

    def layer(side, pad):
        return pl.ds(pad + (EDGE - 1) * side, EDGE, stride=EDGE)

    def ghost(step, side, comp):
        near = pick(faces[step, 1 - side, comp], side)
        far = pick(ghosts[step, side, comp], side)
        return jnp.where(remote[side], far, near)

    def block_of(y, ahead=0):
        start = (y + 1) * EDGE + ahead
        return pl.ds(start, EDGE)

    zero = jnp.zeros(shape, jnp.float32)
    end = EDGE * EDGE

    for h in range(2):
        for z in range(EDGE):
            at = z * EDGE * EDGE + h * LANES
            turned[0, h, pl.ds(z, SLOTS, stride=EDGE), :] = k_ref[:, at : at + LANES]
        kp[EDGE + h * LANES : EDGE + (h + 1) * LANES] = turned[0, h].T
    for side in range(2):
        faces[0, side, 0] = kp[layer(side, EDGE), :]
    lower, upper = kp[EDGE : 2 * EDGE], kp[end : end + EDGE]
    kp[0:EDGE] = jnp.where(valid[2], pick(upper, 2), lower)
    kp[end + EDGE : end + 2 * EDGE] = jnp.where(valid[3], pick(lower, 3), upper)

    pl.semaphore_wait(barrier, peers - 1)
    send(0, 1)

    def harmonic(a, b):
        return jnp.where(live, 2.0 * a * b / (a + b), 0.0)

    def links(y, carry):
        k = kp[block_of(y), :]
        here = pl.ds(y * EDGE, EDGE)
        link[0, here, :] = harmonic(k, kp[block_of(y, -1), :])
        link[1, here, :] = harmonic(k, kp[block_of(y, 1), :])
        link[2, here, :] = harmonic(k, kp[pl.ds(y * EDGE, EDGE), :])
        link[3, here, :] = harmonic(k, kp[block_of(y + 1), :])
        link[4, here, :] = harmonic(k, jnp.where(first_z & ~valid[4], k, pick(k, 4)))
        link[5, here, :] = harmonic(k, jnp.where(last_z & ~valid[5], k, pick(k, 5)))
        return carry

    lax.fori_loop(0, EDGE, links, 0)
    receive(0, 1)

    for side in range(2):
        own = faces[0, side, 0]
        other = jnp.where(valid[side], ghost(0, side, 0), own)
        link[side, layer(side, 0), :] = harmonic(own, other)

    def begin(y, carry):
        here = pl.ds(y * EDGE, EDGE)
        w = [link[side, here, :] for side in range(6)]
        total = ((((w[0] + w[1]) + w[2]) + w[3]) + w[4]) + w[5]
        d = jnp.where(live, total, 1.0)
        inverse = 1.0 / d
        diag[here, :] = d
        n = [x * inverse for x in w]
        n[4] = jnp.where(first_z & ~valid[4], 0.0, n[4])
        n[5] = jnp.where(last_z & ~valid[5], 0.0, n[5])
        for side in range(6):
            weight[side, here, :] = n[side]
        for comp in range(3):
            field[0, comp, block_of(y), :] = (w[2 * comp + 1] - w[2 * comp]) * inverse
        return carry

    lax.fori_loop(0, EDGE, begin, 0)
    for side in range(2):
        edge_w[side] = jnp.where(valid[side], weight[side, layer(side, 0), :], 0.0)
        weight[side, layer(side, 0), :] = zero
        for comp in range(3):
            faces[1, side, comp] = field[0, comp, layer(side, EDGE), :]
    send(1, 3)

    sums = []
    for j in range(ITERS):
        for comp in range(3):
            field[j, comp, 0:EDGE] = jnp.where(
                valid[2], pick(field[j, comp, end : end + EDGE], 2), 0.0
            )
            field[j, comp, end + EDGE : end + 2 * EDGE] = jnp.where(
                valid[3], pick(field[j, comp, EDGE : 2 * EDGE], 3), 0.0
            )

        def inner(y, carry, j=j):
            carry = list(carry)
            here = pl.ds(y * EDGE, EDGE)
            w = [weight[side, here, :] for side in range(6)]
            d = diag[here, :]
            for comp in range(3):
                u = field[j, comp, block_of(y), :]
                value = (
                    (w[0] * field[j, comp, block_of(y, -1), :]
                     + w[1] * field[j, comp, block_of(y, 1), :])
                    + (w[2] * field[j, comp, pl.ds(y * EDGE, EDGE), :]
                       + w[3] * field[j, comp, block_of(y + 1), :])
                    + (w[4] * pick(u, 4) + w[5] * pick(u, 5))
                )
                scaled = d * u
                carry[comp] = carry[comp] + scaled * u
                if j > 0:
                    old = field[j - 1, comp, block_of(y), :]
                    value = 2.0 * value - old
                    carry[3 + comp] = carry[3 + comp] + scaled * old
                field[j + 1, comp, block_of(y), :] = value
            return tuple(carry)

        sums.append(lax.fori_loop(0, EDGE, inner, (zero,) * 6))
        receive(j + 1, 3)
        for side in range(2):
            w = edge_w[side]
            if j > 0:
                w = 2.0 * w
            for comp in range(3):
                extra = jnp.where(valid[side], w * ghost(j + 1, side, comp), 0.0)
                found = field[j + 1, comp, layer(side, EDGE), :] + extra
                field[j + 1, comp, layer(side, EDGE), :] = found
                if j + 1 < ITERS:
                    faces[j + 2, side, comp] = found
        if j + 1 < ITERS:
            send(j + 2, 3)

    def last(y, carry):
        d = diag[pl.ds(y * EDGE, EDGE), :]
        return tuple(
            carry[comp]
            + d * field[ITERS - 1, comp, block_of(y), :] * field[ITERS, comp, block_of(y), :]
            for comp in range(3)
        )

    final = lax.fori_loop(0, EDGE, last, (zero,) * 3)

    def summed(j, odd, comp):
        if not odd:
            return sums[j][comp]
        return sums[j + 1][3 + comp] if j + 1 < ITERS else final[comp]

    shape = (SLOTS, LANES)
    lane = lax.broadcasted_iota(jnp.int32, shape, 1)
    slot = lax.broadcasted_iota(jnp.int32, shape, 0)
    zero = jnp.zeros(shape, jnp.float32)
    mine = zero
    for comp in range(3):
        rows = zero
        for j in range(ITERS):
            for odd in range(2):
                row = jnp.sum(summed(j, odd, comp), axis=0, keepdims=True)
                rows = jnp.where(slot == 2 * j + odd, row, rows)
        mine = jnp.where(lane == comp, jnp.sum(rows, axis=1, keepdims=True), mine)
    moments[...] = mine
    gathered[me] = mine

    def share(offset):
        peer = lax.rem(me + offset, peers)
        return pltpu.make_async_remote_copy(
            src_ref=moments,
            dst_ref=gathered.at[me],
            send_sem=sum_send.at[offset],
            recv_sem=sum_recv.at[me],
            device_id=device(peer),
            device_id_type=MESH,
        )

    def launch(offset, carry):
        share(offset).start()
        return carry

    lax.fori_loop(1, peers, launch, 0)

    def collect(offset, carry):
        source = lax.rem(me + offset, peers)
        share(offset).wait_send()
        pltpu.make_async_remote_copy(
            src_ref=moments,
            dst_ref=gathered.at[source],
            send_sem=sum_send.at[offset],
            recv_sem=sum_recv.at[source],
            device_id=device(source),
            device_id_type=MESH,
        ).wait_recv()
        return carry

    lax.fori_loop(1, peers, collect, 0)
    whole = jnp.sum(gathered[...], axis=0)

    rows = [whole[m : m + 1, :] for m in range(MOMENTS)]
    nu = rows[:2]
    for m in range(2, MOMENTS):
        nu.append(2.0 * rows[m] - rows[m % 2])
    iterate, scaled = cg_coefficients(nu)

    def over(row, comp):
        return jnp.broadcast_to(row[:, comp : comp + 1], (1, LANES))

    for comp in range(3):
        a = [over(row, comp) for row in iterate]
        b = [over(row, comp) for row in scaled]
        for h in range(2):
            inside = pl.ds(EDGE + h * LANES, LANES)
            v = [field[j, comp, inside, :] for j in range(ITERS + 1)]
            d = diag[pl.ds(h * LANES, LANES), :]
            turned[comp, h] = total_of(a[j] * v[j] for j in range(ITERS)).T
            turned[3 + comp, h] = (d * total_of(b[j] * v[j] for j in range(ITERS + 1))).T
            for z in range(EDGE):
                at = z * EDGE * EDGE + h * LANES
                strip = pl.ds(z, SLOTS, stride=EDGE)
                x_ref[comp, :, at : at + LANES] = turned[comp, h, strip, :]
                r_ref[comp, :, at : at + LANES] = turned[3 + comp, h, strip, :]


def local(peers, subs, conductivity, neighbours, live_count):
    slots, voxels = conductivity.shape
    out = jax.ShapeDtypeStruct((3, slots, voxels), jnp.float32)
    vmem = pl.BlockSpec(memory_space=pltpu.VMEM)
    smem = pl.BlockSpec(memory_space=pltpu.SMEM)
    tile = (SLOTS, LANES)
    rows = EDGE * EDGE
    return pl.pallas_call(
        functools.partial(kernel, peers, subs),
        out_shape=(out, out),
        in_specs=[vmem, smem, smem],
        out_specs=(vmem, vmem),
        scratch_shapes=[
            pltpu.VMEM((rows + 2 * EDGE, LANES), jnp.float32),
            pltpu.VMEM((ITERS + 1, 3, rows + 2 * EDGE, LANES), jnp.float32),
            pltpu.VMEM((6, rows, LANES), jnp.float32),
            pltpu.VMEM((rows, LANES), jnp.float32),
            pltpu.VMEM((6, rows, LANES), jnp.float32),
            pltpu.VMEM((ITERS + 1, 2, 3, EDGE, LANES), jnp.float32),
            pltpu.VMEM((ITERS + 1, 2, 3, EDGE, LANES), jnp.float32),
            pltpu.VMEM((2, EDGE, LANES), jnp.float32),
            pltpu.VMEM((6, 2, LANES, LANES), jnp.float32),
            pltpu.VMEM(tile, jnp.float32),
            pltpu.VMEM((peers, *tile), jnp.float32),
            pltpu.SemaphoreType.DMA((ITERS + 1, 2)),
            pltpu.SemaphoreType.DMA((ITERS + 1, 2)),
            pltpu.SemaphoreType.DMA((peers,)),
            pltpu.SemaphoreType.DMA((peers,)),
        ],
        compiler_params=pltpu.CompilerParams(
            collective_id=0, has_side_effects=True, vmem_limit_bytes=24 * 1024 * 1024
        ),
    )(conductivity, neighbours, live_count)


def solution(mesh):
    names = ("ens", "curve", "sub")
    peers = mesh.shape["curve"] * mesh.shape["sub"]
    in_specs = (P(names, None), P(None, names), P(names))
    out_specs = (P(None, names, None), P(None, names, None))
    return jax.shard_map(
        functools.partial(local, peers, mesh.shape["sub"]),
        mesh=mesh, in_specs=in_specs, out_specs=out_specs, check_vma=False,
    )
```

```python
import functools

import jax
import jax.numpy as jnp
from jax import lax
from jax.experimental import pallas as pl
from jax.experimental.pallas import tpu as pltpu
from jax.sharding import PartitionSpec as P

EDGE = 16
ITERS = 4
LANES = 128
SLOTS = 8
MOMENTS = 2 * ITERS
MESH = pl.DeviceIdType.MESH


def total_of(terms):
    terms = list(terms)
    while len(terms) > 1:
        terms = [
            terms[i] + terms[i + 1] if i + 1 < len(terms) else terms[i]
            for i in range(0, len(terms), 2)
        ]
    return terms[0]


def cg_coefficients(nu):
    def gram(i, j):
        return 0.5 * (nu[i + j] + nu[abs(i - j)])

    def pair(a, b):
        return total_of(x * y * gram(i, j) for i, x in enumerate(a) for j, y in enumerate(b))

    def image_of(p):
        q = list(p) + [jnp.zeros_like(p[0])]
        for j, x in enumerate(p):
            if j == 0:
                q[1] = q[1] - x
            else:
                q[j + 1] = q[j + 1] - 0.5 * x
                q[j - 1] = q[j - 1] - 0.5 * x
        return q

    scaled = [jnp.ones_like(nu[0])]
    direction = list(scaled)
    iterate = []
    current = nu[0]
    for step in range(ITERS):
        image = image_of(direction)
        alpha = current / pair(direction, image)
        iterate = [
            (iterate[i] + alpha * x) if i < len(iterate) else alpha * x
            for i, x in enumerate(direction)
        ]
        scaled = [
            (scaled[i] - alpha * x) if i < len(scaled) else -alpha * x
            for i, x in enumerate(image)
        ]
        if step + 1 < ITERS:
            fresh = pair(scaled, scaled)
            beta = fresh / current
            direction = [
                x + beta * direction[i] if i < len(direction) else x
                for i, x in enumerate(scaled)
            ]
            current = fresh
    return iterate, scaled


def kernel(
    peers, subs, k_ref, nb_ref, live_ref, x_ref, r_ref,
    kp, field, weight, diag, link, faces, ghosts, edge_w, turned, moments, gathered,
    face_send, face_recv, sum_send, sum_recv,
):
    me = lax.axis_index("curve") * subs + lax.axis_index("sub")

    def device(index):
        return {"curve": index // subs, "sub": lax.rem(index, subs)}

    barrier = pltpu.get_barrier_semaphore()

    def greet(offset, carry):
        pl.semaphore_signal(
            barrier, inc=1, device_id=device(lax.rem(me + offset, peers)), device_id_type=MESH
        )
        return carry

    lax.fori_loop(1, peers, greet, 0)

    shape = (EDGE, LANES)
    lane = lax.broadcasted_iota(jnp.int32, shape, 1)
    row = lax.broadcasted_iota(jnp.int32, shape, 0)
    depth = lane % EDGE
    owner = lane // EDGE
    first_x, last_x = row == 0, row == EDGE - 1
    first_z, last_z = depth == 0, depth == EDGE - 1
    live = owner < live_ref[0]
    index, valid, remote = [], [], []
    for side in range(6):
        entry = jnp.full(shape, nb_ref[side, 0], jnp.int32)
        for s in range(1, SLOTS):
            entry = jnp.where(owner == s, nb_ref[side, s], entry)
        valid.append(entry >= 0)
        index.append(jnp.where(valid[side], entry % SLOTS, 0) * EDGE)
        if side < 2:
            remote.append(
                valid[side] & ((entry < me * SLOTS) | (entry >= (me + 1) * SLOTS))
            )
    for side in range(4):
        index[side] = index[side] + depth
    index[4] = jnp.where(first_z, index[4] + (EDGE - 1), lane - 1)
    index[5] = jnp.where(last_z, index[5], lane + 1)

    def pick(block, side):
        where = index[side]
        return jnp.concatenate(
            [
                jnp.take_along_axis(
                    block[h : h + 8], where[h : h + 8], axis=1, mode="promise_in_bounds"
                )
                for h in range(0, EDGE, 8)
            ],
            axis=0,
        )

    def copies(step, width):
        def make(side, peer):
            span = pl.ds(0, width)
            return pltpu.make_async_remote_copy(
                src_ref=faces.at[step, side, span],
                dst_ref=ghosts.at[step, 1 - side, span],
                send_sem=face_send.at[step, side],
                recv_sem=face_recv.at[step, 1 - side],
                device_id=device(peer),
                device_id_type=MESH,
            )

        return make(0, jnp.maximum(me - 1, 0)), make(1, jnp.minimum(me + 1, peers - 1))

    def send(step, width):
        down, up = copies(step, width)

        @pl.when(me > 0)
        def _():
            down.start()

        @pl.when(me < peers - 1)
        def _():
            up.start()

    def receive(step, width):
        down, up = copies(step, width)

        @pl.when(me < peers - 1)
        def _():
            down.wait_recv()
            up.wait_send()

        @pl.when(me > 0)
        def _():
            up.wait_recv()
            down.wait_send()

    def layer(side, pad):
        return pl.ds(pad + (EDGE - 1) * side, EDGE, stride=EDGE)

    def ghost(step, side, comp):
        near = pick(faces[step, 1 - side, comp], side)
        far = pick(ghosts[step, side, comp], side)
        return jnp.where(remote[side], far, near)

    def block_of(y, ahead=0):
        start = (y + 1) * EDGE + ahead
        return pl.ds(start, EDGE)

    zero = jnp.zeros(shape, jnp.float32)
    end = EDGE * EDGE

    for h in range(2):
        for z in range(EDGE):
            at = z * EDGE * EDGE + h * LANES
            turned[0, h, pl.ds(z, SLOTS, stride=EDGE), :] = k_ref[:, at : at + LANES]
        kp[EDGE + h * LANES : EDGE + (h + 1) * LANES] = turned[0, h].T
    for side in range(2):
        faces[0, side, 0] = kp[layer(side, EDGE), :]
    lower, upper = kp[EDGE : 2 * EDGE], kp[end : end + EDGE]
    kp[0:EDGE] = jnp.where(valid[2], pick(upper, 2), lower)
    kp[end + EDGE : end + 2 * EDGE] = jnp.where(valid[3], pick(lower, 3), upper)

    pl.semaphore_wait(barrier, peers - 1)
    send(0, 1)

    def harmonic(a, b):
        return jnp.where(live, 2.0 * a * b / (a + b), 0.0)

    def links(y, carry):
        k = kp[block_of(y), :]
        here = pl.ds(y * EDGE, EDGE)
        link[0, here, :] = harmonic(k, kp[block_of(y, -1), :])
        link[1, here, :] = harmonic(k, kp[block_of(y, 1), :])
        link[2, here, :] = harmonic(k, kp[pl.ds(y * EDGE, EDGE), :])
        link[3, here, :] = harmonic(k, kp[block_of(y + 1), :])
        link[4, here, :] = harmonic(k, jnp.where(first_z & ~valid[4], k, pick(k, 4)))
        link[5, here, :] = harmonic(k, jnp.where(last_z & ~valid[5], k, pick(k, 5)))
        return carry

    lax.fori_loop(0, EDGE, links, 0, unroll=True)
    receive(0, 1)

    for side in range(2):
        own = faces[0, side, 0]
        other = jnp.where(valid[side], ghost(0, side, 0), own)
        link[side, layer(side, 0), :] = harmonic(own, other)

    def begin(y, carry):
        here = pl.ds(y * EDGE, EDGE)
        w = [link[side, here, :] for side in range(6)]
        total = ((((w[0] + w[1]) + w[2]) + w[3]) + w[4]) + w[5]
        d = jnp.where(live, total, 1.0)
        inverse = 1.0 / d
        diag[here, :] = d
        n = [x * inverse for x in w]
        n[4] = jnp.where(first_z & ~valid[4], 0.0, n[4])
        n[5] = jnp.where(last_z & ~valid[5], 0.0, n[5])
        for side in range(6):
            weight[side, here, :] = n[side]
        for comp in range(3):
            field[0, comp, block_of(y), :] = (w[2 * comp + 1] - w[2 * comp]) * inverse
        return carry

    lax.fori_loop(0, EDGE, begin, 0, unroll=True)
    for side in range(2):
        edge_w[side] = jnp.where(valid[side], weight[side, layer(side, 0), :], 0.0)
        weight[side, layer(side, 0), :] = zero
        for comp in range(3):
            faces[1, side, comp] = field[0, comp, layer(side, EDGE), :]
    send(1, 3)

    sums = []
    for j in range(ITERS):
        for comp in range(3):
            field[j, comp, 0:EDGE] = jnp.where(
                valid[2], pick(field[j, comp, end : end + EDGE], 2), 0.0
            )
            field[j, comp, end + EDGE : end + 2 * EDGE] = jnp.where(
                valid[3], pick(field[j, comp, EDGE : 2 * EDGE], 3), 0.0
            )

        def inner(y, carry, j=j):
            carry = list(carry)
            here = pl.ds(y * EDGE, EDGE)
            w = [weight[side, here, :] for side in range(6)]
            d = diag[here, :]
            for comp in range(3):
                u = field[j, comp, block_of(y), :]
                value = (
                    (w[0] * field[j, comp, block_of(y, -1), :]
                     + w[1] * field[j, comp, block_of(y, 1), :])
                    + (w[2] * field[j, comp, pl.ds(y * EDGE, EDGE), :]
                       + w[3] * field[j, comp, block_of(y + 1), :])
                    + (w[4] * pick(u, 4) + w[5] * pick(u, 5))
                )
                scaled = d * u
                carry[comp] = carry[comp] + scaled * u
                if j > 0:
                    old = field[j - 1, comp, block_of(y), :]
                    value = 2.0 * value - old
                    carry[3 + comp] = carry[3 + comp] + scaled * old
                field[j + 1, comp, block_of(y), :] = value
            return tuple(carry)

        sums.append(lax.fori_loop(0, EDGE, inner, (zero,) * 6, unroll=True))
        receive(j + 1, 3)
        for side in range(2):
            w = edge_w[side]
            if j > 0:
                w = 2.0 * w
            for comp in range(3):
                extra = jnp.where(valid[side], w * ghost(j + 1, side, comp), 0.0)
                found = field[j + 1, comp, layer(side, EDGE), :] + extra
                field[j + 1, comp, layer(side, EDGE), :] = found
                if j + 1 < ITERS:
                    faces[j + 2, side, comp] = found
        if j + 1 < ITERS:
            send(j + 2, 3)

    def last(y, carry):
        d = diag[pl.ds(y * EDGE, EDGE), :]
        return tuple(
            carry[comp]
            + d * field[ITERS - 1, comp, block_of(y), :] * field[ITERS, comp, block_of(y), :]
            for comp in range(3)
        )

    final = lax.fori_loop(0, EDGE, last, (zero,) * 3, unroll=True)

    def summed(j, odd, comp):
        if not odd:
            return sums[j][comp]
        return sums[j + 1][3 + comp] if j + 1 < ITERS else final[comp]

    shape = (SLOTS, LANES)
    lane = lax.broadcasted_iota(jnp.int32, shape, 1)
    slot = lax.broadcasted_iota(jnp.int32, shape, 0)
    zero = jnp.zeros(shape, jnp.float32)
    mine = zero
    for comp in range(3):
        rows = zero
        for j in range(ITERS):
            for odd in range(2):
                row = jnp.sum(summed(j, odd, comp), axis=0, keepdims=True)
                rows = jnp.where(slot == 2 * j + odd, row, rows)
        mine = jnp.where(lane == comp, jnp.sum(rows, axis=1, keepdims=True), mine)
    moments[...] = mine
    gathered[me] = mine

    def share(offset):
        peer = lax.rem(me + offset, peers)
        return pltpu.make_async_remote_copy(
            src_ref=moments,
            dst_ref=gathered.at[me],
            send_sem=sum_send.at[offset],
            recv_sem=sum_recv.at[me],
            device_id=device(peer),
            device_id_type=MESH,
        )

    def launch(offset, carry):
        share(offset).start()
        return carry

    lax.fori_loop(1, peers, launch, 0)

    def collect(offset, carry):
        source = lax.rem(me + offset, peers)
        share(offset).wait_send()
        pltpu.make_async_remote_copy(
            src_ref=moments,
            dst_ref=gathered.at[source],
            send_sem=sum_send.at[offset],
            recv_sem=sum_recv.at[source],
            device_id=device(source),
            device_id_type=MESH,
        ).wait_recv()
        return carry

    lax.fori_loop(1, peers, collect, 0)
    whole = jnp.sum(gathered[...], axis=0)

    rows = [whole[m : m + 1, :] for m in range(MOMENTS)]
    nu = rows[:2]
    for m in range(2, MOMENTS):
        nu.append(2.0 * rows[m] - rows[m % 2])
    iterate, scaled = cg_coefficients(nu)

    def over(row, comp):
        return jnp.broadcast_to(row[:, comp : comp + 1], (1, LANES))

    for comp in range(3):
        a = [over(row, comp) for row in iterate]
        b = [over(row, comp) for row in scaled]
        for h in range(2):
            inside = pl.ds(EDGE + h * LANES, LANES)
            v = [field[j, comp, inside, :] for j in range(ITERS + 1)]
            d = diag[pl.ds(h * LANES, LANES), :]
            turned[comp, h] = total_of(a[j] * v[j] for j in range(ITERS)).T
            turned[3 + comp, h] = (d * total_of(b[j] * v[j] for j in range(ITERS + 1))).T
            for z in range(EDGE):
                at = z * EDGE * EDGE + h * LANES
                strip = pl.ds(z, SLOTS, stride=EDGE)
                x_ref[comp, :, at : at + LANES] = turned[comp, h, strip, :]
                r_ref[comp, :, at : at + LANES] = turned[3 + comp, h, strip, :]


def local(peers, subs, conductivity, neighbours, live_count):
    slots, voxels = conductivity.shape
    out = jax.ShapeDtypeStruct((3, slots, voxels), jnp.float32)
    vmem = pl.BlockSpec(memory_space=pltpu.VMEM)
    smem = pl.BlockSpec(memory_space=pltpu.SMEM)
    tile = (SLOTS, LANES)
    rows = EDGE * EDGE
    return pl.pallas_call(
        functools.partial(kernel, peers, subs),
        out_shape=(out, out),
        in_specs=[vmem, smem, smem],
        out_specs=(vmem, vmem),
        scratch_shapes=[
            pltpu.VMEM((rows + 2 * EDGE, LANES), jnp.float32),
            pltpu.VMEM((ITERS + 1, 3, rows + 2 * EDGE, LANES), jnp.float32),
            pltpu.VMEM((6, rows, LANES), jnp.float32),
            pltpu.VMEM((rows, LANES), jnp.float32),
            pltpu.VMEM((6, rows, LANES), jnp.float32),
            pltpu.VMEM((ITERS + 1, 2, 3, EDGE, LANES), jnp.float32),
            pltpu.VMEM((ITERS + 1, 2, 3, EDGE, LANES), jnp.float32),
            pltpu.VMEM((2, EDGE, LANES), jnp.float32),
            pltpu.VMEM((6, 2, LANES, LANES), jnp.float32),
            pltpu.VMEM(tile, jnp.float32),
            pltpu.VMEM((peers, *tile), jnp.float32),
            pltpu.SemaphoreType.DMA((ITERS + 1, 2)),
            pltpu.SemaphoreType.DMA((ITERS + 1, 2)),
            pltpu.SemaphoreType.DMA((peers,)),
            pltpu.SemaphoreType.DMA((peers,)),
        ],
        compiler_params=pltpu.CompilerParams(
            collective_id=0, has_side_effects=True, vmem_limit_bytes=24 * 1024 * 1024
        ),
    )(conductivity, neighbours, live_count)


def solution(mesh):
    names = ("ens", "curve", "sub")
    peers = mesh.shape["curve"] * mesh.shape["sub"]
    in_specs = (P(names, None), P(None, names), P(names))
    out_specs = (P(None, names, None), P(None, names, None))
    return jax.shard_map(
        functools.partial(local, peers, mesh.shape["sub"]),
        mesh=mesh, in_specs=in_specs, out_specs=out_specs, check_vma=False,
    )
```
